32 devices in a mesh: mem: 4 (over y, x), dom: 8 (over z, core).
Axes of the slice: x: 2, y: 2, z: 4, core: 2. Of those that a mesh axis runs over, the one named last changes fastest.
Arguments:
- sample_vectors_prior: float32 [16, 5, 256, 256], P('mem', None, 'dom'), may hold values from -6 to 6
- smoothing_number: float32 [5, 256, 256], P(None, 'dom'), may hold values from 0.02 to 0.2
- cross_quantity_factor: float32 [5, 5], replicated, may hold values from -0.6 to 0.6
- obs_tile: int32 [2, 2048, 1], replicated, may hold values from 0 to 7; in each aligned block of 2048 rows (0 to 2047, 2048 to 4095, ..., all dimensions but the last counted through in order) at most 512 rows name the same one
- measured_gridpoint: int32 [2, 2048], replicated, may hold values from 0 to 7904
- obs_field: int32 [2, 2048], replicated, may hold values from 0 to 4
- obs_weights: float32 [2, 2048, 4], replicated, may hold values from 0.1 to 0.5
- obs_values: float32 [2, 2048], replicated, may hold values from -8 to 8
- observation_variance: float32 [2, 2048], replicated, may hold values from 0.2 to 2
- localization: float32 [2, 8, 2048], P(None, 'dom'), may hold values from 0.001 to 0.02
Outputs:
- analysis: float32 [16, 5, 256, 256], P('mem', None, 'dom')
The draws below stay inside these ranges and needn't reach their ends.
Inputs may be any that keep to these rules, and one draw needn't show every extreme that they name: `obs_tile`: in each batch at most 512 observations share an owning tile, and in some batch some tile owns exactly 512. Local row measured_gridpoint // 255, column measured_gridpoint % 255; the four points used lie in the owning tile.
All inputs are finite; a program needn't handle non-finite values.
Results may differ from the reference program's by a relative error of at most 0.0001.
Values sent between devices are 32-bit elements; how exact they have to be, the bound alone decides.
A program may use at most 128 MiB of HBM per device.

```python
import math
import jax
import jax.numpy as jnp
import numpy as np
from jax import lax

F = 5
CX = 32
GY = 256
STEPS = 2
BATCHES = 2
NOBS = 2048
TILES = 8
MEMBERS = 16
NX = 256
CAP = 512


def with_ends(values, own_key, least, largest):
    spot = [jax.random.randint(jax.random.fold_in(own_key, axis), (), 0, length) for axis, length in enumerate(values.shape)]
    widest = values.shape.index(max(values.shape))
    beside = spot[:widest] + [(spot[widest] + 1) % values.shape[widest]] + spot[widest + 1:]
    return values.at[tuple(spot)].set(least).at[tuple(beside)].set(largest)


def block_scale(key, dims, shards, smallest, high):
    def one(axis_at, shards_of):
        heights = jax.random.uniform(jax.random.fold_in(jax.random.fold_in(key, 6), axis_at), (shards_of,), jnp.float32, smallest / len(shards), high / len(shards))
        return jnp.repeat(jnp.exp(heights), dims[axis_at] // shards_of).reshape((-1,) + (1,) * (len(dims) - axis_at - 1))

    level = one(*shards[0])
    for cut in shards[1:]:
        level = level * one(*cut)
    return level


def assign_block(stream_key, own, number, rows, amount, top, most, skew):
    sequence = jax.random.permutation(stream_key, amount)
    heavy_load, common = shares(amount, rows * top, most, skew, True), shares(amount, rows * top, most, skew, False)
    places = jnp.arange(amount)

    def named(lengths, rotation):
        used = int((lengths > 0).sum())
        fixed = max(1, used // 4)
        shifted = fixed + (places - fixed + rotation * (used - fixed)) % max(1, amount - fixed)
        return jnp.zeros((amount,), jnp.int32).at[sequence[jnp.where(places < fixed, places, shifted)]].set(jnp.asarray(lengths, jnp.int32))

    lengths = jnp.where(number % 4 == 0, named(heavy_load, number // 4), named(common, number - number // 4 - 1))
    mixed = jax.random.permutation(jax.random.fold_in(own, 3), amount)
    source_of, sink = mixed[0:amount // 2 * 2:2], mixed[1:amount // 2 * 2:2]
    margin = jnp.minimum(lengths[source_of] - 1, most - lengths[sink]) // 2
    margin = jnp.where((source_of == sequence[0]) | (sink == sequence[0]) | (lengths[sink] == 0), 0, jnp.maximum(margin, 0))
    shifted = jax.random.randint(jax.random.fold_in(own, 4), (amount // 2,), 0, 1 << 20) % (margin + 1)
    lengths = lengths.at[source_of].add(-shifted).at[sink].add(shifted)
    members = jnp.searchsorted(jnp.cumsum(lengths), jnp.arange(rows * top), side="right").astype(jnp.int32)
    table = members.reshape(top, rows).T
    table = table[jax.random.permutation(jax.random.fold_in(own, 1), rows)]
    rotation = jax.random.randint(jax.random.fold_in(own, 2), (rows, 1), 0, top)
    return jnp.take_along_axis(table, (jnp.arange(top)[None, :] + rotation) % top, axis=1)


def shares(amount, total, reach, skew, full):
    portions = [(1 << 20) // math.isqrt(rank ** skew) + 1 for rank in range(1, amount + 1)]
    largest = reach if full else min(reach, max(-(-total // amount), total * portions[0] // sum(portions)))
    least = 1 if total - largest >= amount - 1 else 0
    given, rest = [largest] + [least] * (amount - 1), total - largest - least * (amount - 1)
    while rest > 0:
        candidates = [i for i in range(1, amount) if given[i] < largest] or [i for i in range(1, amount) if given[i] < reach]
        whole, left = sum([portions[i] for i in candidates]), rest
        for i in candidates:
            addition = min(reach - given[i], max(1, left * portions[i] // whole), rest)
            given[i] = given[i] + addition
            rest = rest - addition
    return np.array(given)


def normal_values(key, extent, width, bound, cuts=(), kind=jnp.bfloat16):
    drawn = jax.random.normal(key, extent, jnp.float32) * width
    if len(cuts) > 0:
        drawn = block_scale(key, extent, cuts, -0.22, 0.18) * drawn
    return jnp.clip(drawn, min=-bound, max=bound).astype(kind)


def setup_inputs(seed: int = 0) -> dict:
    key_list = jax.random.split(jax.random.key(seed), 11)
    sample_vectors_prior = normal_values(key_list[0], (MEMBERS, F, NX, GY), 1.0, 6.0, ((0, 4), (2, 8)), jnp.float32)
    smoothing_number = jnp.clip(jnp.exp(math.log(0.2) - 2.3025851 * jax.random.uniform(key_list[1], (F, NX, GY), jnp.float32) ** block_scale(key_list[1], (F, NX, GY), ((1, 8),), -0.2, 0.2)), 0.02, 0.2)
    cross_quantity_factor = normal_values(key_list[2], (F, F), 0.15, 0.6, (), jnp.float32)
    obs_tile_keys = jax.random.split(jax.random.fold_in(key_list[3], 1), BATCHES * NOBS // NOBS)
    obs_tile_turns = jax.random.permutation(jax.random.fold_in(key_list[3], 3), BATCHES * NOBS // NOBS)
    obs_tile = jax.vmap(lambda own, number: assign_block(jax.random.fold_in(key_list[3], 2), own, number, NOBS, TILES, 1, CAP, 2))(obs_tile_keys, obs_tile_turns).reshape((BATCHES, NOBS, 1))
    measured_gridpoint = with_ends(jax.random.randint(key_list[4], (BATCHES, NOBS), 0, (CX - 1) * (GY - 1)), jax.random.fold_in(key_list[4], 1), 0, ((CX - 1) * (GY - 1)) - 1).astype(jnp.int32)
    obs_field = with_ends(jax.random.randint(key_list[5], (BATCHES, NOBS), 0, F), jax.random.fold_in(key_list[5], 1), 0, F - 1).astype(jnp.int32)
    obs_weights = jnp.clip(jax.random.uniform(key_list[6], (BATCHES, NOBS, 4), jnp.float32, 0.1, 0.5), 0.1, 0.5)
    obs_values = normal_values(key_list[7], (BATCHES, NOBS), 1.5, 8.0, (), jnp.float32)
    observation_variance = jnp.clip(jnp.exp(jax.random.uniform(key_list[8], (BATCHES, NOBS), jnp.float32, math.log(0.2), math.log(2.0))), 0.2, 2.0)
    localization = jnp.clip(jnp.exp(math.log(0.02) - 2.9957322 * jax.random.uniform(key_list[9], (BATCHES, TILES, NOBS), jnp.float32) ** block_scale(key_list[9], (BATCHES, TILES, NOBS), ((1, 8),), -0.2, 0.2)), 0.001, 0.02)
    return dict(sample_vectors_prior=sample_vectors_prior, smoothing_number=smoothing_number, cross_quantity_factor=cross_quantity_factor, obs_tile=obs_tile, measured_gridpoint=measured_gridpoint, obs_field=obs_field, obs_weights=obs_weights, obs_values=obs_values, observation_variance=observation_variance, localization=localization)


def predicted_quantity(sample_vectors_prior, smoothing_number, cross_quantity_factor):
    padded = jnp.pad(sample_vectors_prior, ((0, 0), (0, 0), (1, 1), (1, 1)))
    lap = padded[:, :, 2:, 1:-1] + padded[:, :, :-2, 1:-1]
    lap = lap + padded[:, :, 1:-1, 2:] + padded[:, :, 1:-1, :-2] - 4.0 * sample_vectors_prior
    mixed = jnp.einsum('fg,mgxy->mfxy', cross_quantity_factor, sample_vectors_prior, precision=lax.Precision.HIGHEST)
    return sample_vectors_prior + smoothing_number[None] * lap + mixed

def reference(sample_vectors_prior, smoothing_number, cross_quantity_factor, obs_tile, measured_gridpoint, obs_field, obs_weights, obs_values, observation_variance, localization):
    for step_index in range(STEPS):
        sample_vectors_prior = predicted_quantity(sample_vectors_prior, smoothing_number, cross_quantity_factor)
    for batch_index in range(BATCHES):
        owner = obs_tile[batch_index, :, 0].astype(jnp.int32)
        place = measured_gridpoint[batch_index].astype(jnp.int32)
        row_local = place // (GY - 1)
        column = place % (GY - 1)
        base = obs_field[batch_index].astype(jnp.int32) * (NX * GY) + (owner * CX + row_local) * GY + column
        offsets = jnp.array([0, 1, GY, GY + 1], dtype=jnp.int32)
        points = (base[:, None] + offsets[None, :]).reshape(-1)
        flat = sample_vectors_prior.reshape(MEMBERS, F * NX * GY)
        values = jnp.take(flat, points, axis=1).reshape(MEMBERS, NOBS, 4)
        prior = lax.optimization_barrier(jnp.sum(values * obs_weights[batch_index][None], axis=-1))
        mean_prior = lax.optimization_barrier(jnp.mean(prior, axis=0))
        ensemble_spread = prior - mean_prior[None]
        variance = lax.optimization_barrier(jnp.sum(ensemble_spread * ensemble_spread, axis=0)) / (MEMBERS - 1)
        error = observation_variance[batch_index]
        total = variance + error
        gain = (obs_values[batch_index] - mean_prior)[None] / total[None] - ensemble_spread / (jnp.sqrt(total) * (jnp.sqrt(error) + jnp.sqrt(total)))[None]
        mixing = jnp.einsum('mo,to,no->tmn', ensemble_spread, localization[batch_index], gain, precision=lax.Precision.HIGHEST) / (MEMBERS - 1)
        tiles = sample_vectors_prior.reshape(MEMBERS, F, TILES, CX, GY)
        anomaly = tiles - lax.optimization_barrier(jnp.mean(tiles, axis=0))[None]
        tiles = tiles + jnp.einsum('mftxy,tmn->nftxy', anomaly, mixing, precision=lax.Precision.HIGHEST)
        sample_vectors_prior = tiles.reshape(MEMBERS, F, NX, GY)
    return sample_vectors_prior
```

```python
import functools

import jax
import jax.numpy as jnp
from jax import lax
from jax.experimental import pallas as pl
from jax.experimental.pallas import tpu as pltpu
from jax.sharding import PartitionSpec as P

STEPS = 2
HALO = 8
MESH = pl.DeviceIdType.MESH
HIGHEST = lax.Precision.HIGHEST
F32 = jnp.float32
BF16 = jnp.bfloat16


def three_parts(a):
    high = a.astype(BF16).astype(F32)
    rest = a - high
    middle = rest.astype(BF16).astype(F32)
    return jnp.concatenate([high, middle, rest - middle], axis=0).astype(BF16)


def iota(shape, dim):
    return lax.broadcasted_iota(jnp.int32, shape, dim)


def kernel(
    nmem, ndom, cap,
    x_ref, s_ref, c_ref, tile_ref, attr_ref, loc_ref,
    out_ref,
    pad, spad, xu, xh, xl, pick, comp, csel, rsel, lbuf, lrow, lcomp,
    pbuf, xg, og, og_in, ps, rb, wb,
    local_sem, halo_send, halo_recv, loc_send, loc_recv, pri_send, pri_recv,
    st_send, st_recv, mix_send, mix_recv, fin_send, fin_recv,
):
    me = lax.axis_index("mem")
    tile = lax.axis_index("dom")
    own, fields, rows, cols = x_ref.shape
    members = own * nmem
    batches, _, nobs = attr_ref.shape
    wide = xu.shape[-1]
    across = cols // wide
    lane_blocks = nobs // 128
    last = ndom - 1

    load_x = pltpu.make_async_copy(x_ref, pad.at[:, :, HALO:HALO + rows, :], local_sem.at[0])
    load_s = pltpu.make_async_copy(s_ref, spad.at[:, HALO:HALO + rows, :], local_sem.at[1])
    load_x.start()
    load_s.start()

    barrier = pltpu.get_barrier_semaphore()
    for d in range(1, nmem):
        pl.semaphore_signal(barrier, inc=1, device_id={"mem": lax.rem(me + d, nmem)}, device_id_type=MESH)
    for d in range(1, ndom):
        pl.semaphore_signal(barrier, inc=1, device_id={"dom": lax.rem(tile + d, ndom)}, device_id_type=MESH)

    @pl.when(tile == 0)
    def _():
        pad[:, :, 0:HALO, :] = jnp.zeros((own, fields, HALO, cols), F32)
        spad[:, 0:HALO, :] = jnp.zeros((fields, HALO, cols), F32)

    @pl.when(tile == last)
    def _():
        pad[:, :, HALO + rows:, :] = jnp.zeros((own, fields, HALO, cols), F32)
        spad[:, HALO + rows:, :] = jnp.zeros((fields, HALO, cols), F32)

    pl.semaphore_wait(barrier, nmem + ndom - 2)

    def halo(src, dst, to, slot):
        return pltpu.make_async_remote_copy(
            src_ref=src, dst_ref=dst, send_sem=halo_send.at[slot], recv_sem=halo_recv.at[slot],
            device_id={"dom": to}, device_id_type=MESH,
        )

    below = lax.rem(tile + ndom - 1, ndom)
    above = lax.rem(tile + 1, ndom)
    down = [
        halo(x_ref.at[:, :, 0:HALO, :], pad.at[:, :, HALO + rows:HALO + rows + HALO, :], below, 0),
        halo(s_ref.at[:, 0:HALO, :], spad.at[:, HALO + rows:HALO + rows + HALO, :], below, 1),
    ]
    up = [
        halo(x_ref.at[:, :, rows - HALO:rows, :], pad.at[:, :, 0:HALO, :], above, 2),
        halo(s_ref.at[:, rows - HALO:rows, :], spad.at[:, 0:HALO, :], above, 3),
    ]

    @pl.when(tile > 0)
    def _():
        for copy in down:
            copy.start()

    @pl.when(tile < last)
    def _():
        for copy in up:
            copy.start()

    loc_copies = []
    for d in range(1, ndom):
        copy = pltpu.make_async_remote_copy(
            src_ref=loc_ref, dst_ref=lbuf.at[tile], send_sem=loc_send.at[d], recv_sem=loc_recv.at[d],
            device_id={"dom": lax.rem(tile + d, ndom)}, device_id_type=MESH,
        )
        copy.start()
        loc_copies.append(copy)
    lbuf[tile] = loc_ref[...]

    count = batches * lane_blocks
    owned = tile_ref[...] == tile
    ownf = jnp.where(owned, 1.0, 0.0).astype(F32)
    ahead = jnp.where(iota((128, 128), 0) < iota((128, 128), 1), 1.0, 0.0).astype(BF16)
    row_i, row_j = iota((count, count), 0), iota((count, count), 1)
    prior_rows = jnp.where((row_j < row_i) & (row_j // lane_blocks == row_i // lane_blocks), 1.0, 0.0).astype(BF16)
    within = jnp.dot(ownf.astype(BF16), ahead, preferred_element_type=F32)
    offset = jnp.sum(jnp.dot(prior_rows, ownf.astype(BF16), preferred_element_type=F32), axis=1, keepdims=True)
    rank = jnp.where(owned, within + offset, -1.0)
    rank = jnp.concatenate([rank, jnp.full((128 - count, 128), -1.0, F32)], axis=0) if count < 128 else rank
    rank_t = jnp.transpose(rank)
    slots = iota((128, cap), 1).astype(F32)
    for b in range(batches):
        for k in range(lane_blocks):
            at = b * lane_blocks + k
            pick[b, k * 128:(k + 1) * 128, :] = jnp.where(rank_t[:, at:at + 1] == slots, 1.0, 0.0).astype(BF16)
    for b in range(batches):
        got = jnp.dot(three_parts(attr_ref[b]), pick[b], preferred_element_type=F32)
        packed = got[0:8] + got[8:16] + got[16:24]
        comp[b] = packed
        column = packed[1:2, :].astype(jnp.int32)
        line = packed[0:1, :].astype(jnp.int32)
        col_at = iota((cols, cap), 0)
        csel[b, 0] = jnp.where(col_at == column, 1.0, 0.0).astype(BF16)
        csel[b, 1] = jnp.where(col_at == column + 1, 1.0, 0.0).astype(BF16)
        line_at = iota((fields * rows, cap), 0)
        here, after = line_at == line, line_at == line + 1
        rsel[b, 0] = jnp.where(here, packed[2:3, :], jnp.where(after, packed[4:5, :], 0.0))
        rsel[b, 1] = jnp.where(here, packed[3:4, :], jnp.where(after, packed[5:6, :], 0.0))

    load_x.wait()
    load_s.wait()

    @pl.when(tile > 0)
    def _():
        for copy in up:
            copy.wait_recv()

    @pl.when(tile < last)
    def _():
        for copy in down:
            copy.wait_recv()

    height = rows + 2 * HALO
    lane = iota((height, cols), 1)

    def member(m, carry):
        x = [pad[m, f] for f in range(fields)]
        for _ in range(STEPS):
            new = []
            for f in range(fields):
                v = x[f]
                lap = pltpu.roll(v, 1, 0) + pltpu.roll(v, height - 1, 0)
                lap = lap + jnp.where(lane < cols - 1, pltpu.roll(v, cols - 1, 1), 0.0)
                lap = lap + jnp.where(lane > 0, pltpu.roll(v, 1, 1), 0.0) - 4.0 * v
                mixed = c_ref[f, 0] * x[0]
                for g in range(1, fields):
                    mixed = mixed + c_ref[f, g] * x[g]
                new.append(v + spad[f] * lap + mixed)
            x = new
        for f in range(fields):
            v = x[f][HALO:HALO + rows]
            high = v.astype(BF16)
            xh[m, f * rows:(f + 1) * rows, :] = high
            xl[m, f * rows:(f + 1) * rows, :] = (v - high.astype(F32)).astype(BF16)
            for k in range(nmem):
                r, c = k // across * 8, k % across * wide
                xu[k, m, f] = v[r:r + 8, c:c + wide]
        return carry

    lax.fori_loop(0, own, member, 0)

    def observe(m, carry):
        for b in range(batches):
            total = jnp.zeros((1, cap), F32)
            for side in range(2):
                t = jnp.dot(xh[m], csel[b, side], preferred_element_type=F32)
                t = t + jnp.dot(xl[m], csel[b, side], preferred_element_type=F32)
                total = total + jnp.sum(t * rsel[b, side], axis=0, keepdims=True)
            pbuf[me, m, :, b * cap:(b + 1) * cap] = total
        return carry

    lax.fori_loop(0, own, observe, 0)
    pri_copies = []
    for d in range(1, nmem):
        copy = pltpu.make_async_remote_copy(
            src_ref=pbuf.at[me], dst_ref=pbuf.at[me], send_sem=pri_send.at[d], recv_sem=pri_recv.at[d],
            device_id={"mem": lax.rem(me + d, nmem)}, device_id_type=MESH,
        )
        copy.start()
        pri_copies.append(copy)
    st_copies = []
    for d in range(1, nmem):
        to = lax.rem(me + d, nmem)
        copy = pltpu.make_async_remote_copy(
            src_ref=xu.at[to], dst_ref=xg.at[me], send_sem=st_send.at[d], recv_sem=st_recv.at[d],
            device_id={"mem": to}, device_id_type=MESH,
        )
        copy.start()
        st_copies.append(copy)
    xg[me] = xu[me]

    for copy in loc_copies:
        copy.wait_recv()
    for t in range(ndom):
        lrow[t:t + 1, :] = lbuf[t]
    for b in range(batches):
        got = jnp.dot(
            three_parts(lrow[:, b * nobs:(b + 1) * nobs]), pick[b], preferred_element_type=F32
        )
        lcomp[b] = got[0:ndom] + got[ndom:2 * ndom] + got[2 * ndom:3 * ndom]

    for copy in pri_copies:
        copy.wait_recv()

    def gather_prior(b):
        return jnp.concatenate(
            [pbuf[i, m, :, b * cap:(b + 1) * cap] for i in range(nmem) for m in range(own)], axis=0
        )

    def mixing_of(b, prior):
        value = comp[b, 6:7, :]
        error = comp[b, 7:8, :]
        error = jnp.where(error > 0.0, error, 1.0)
        mean = jnp.sum(prior, axis=0, keepdims=True) / members
        spread = prior - mean
        total = jnp.sum(spread * spread, axis=0, keepdims=True) / (members - 1) + error
        root = jnp.sqrt(total)
        gain = (value - mean) / total - spread / (root * (jnp.sqrt(error) + root))
        local = jnp.concatenate([gain * lcomp[b, t:t + 1, :] for t in range(ndom)], axis=0)
        wide_spread = jnp.concatenate([spread, jnp.zeros((128 - members, cap), F32)], axis=0)
        part = lax.dot_general(
            local, wide_spread, (((1,), (1,)), ((), ())), precision=HIGHEST, preferred_element_type=F32
        ) / (members - 1)
        for t in range(ndom):
            ps[b, t] = part[t * members:(t + 1) * members]
        copies = []
        for d in range(1, ndom):
            to = lax.rem(tile + d, ndom)
            copy = pltpu.make_async_remote_copy(
                src_ref=ps.at[b, to], dst_ref=rb.at[b, tile],
                send_sem=mix_send.at[b, d], recv_sem=mix_recv.at[b, d],
                device_id={"dom": to}, device_id_type=MESH,
            )
            copy.start()
            copies.append(copy)
        rb[b, tile] = ps[b, tile]
        for copy in copies:
            copy.wait_recv()
        return jnp.sum(rb[b], axis=0)[:, 0:members], copies

    eye = jnp.where(iota((members, members), 0) == iota((members, members), 1), 1.0, 0.0).astype(F32)
    mix_copies = []
    advance = eye
    folded = jnp.zeros((members, members), F32)
    for b in range(batches):
        prior = gather_prior(b)
        if b > 0:
            anomaly = prior - jnp.sum(prior, axis=0, keepdims=True) / members
            prior = prior + jnp.dot(folded, anomaly, precision=HIGHEST, preferred_element_type=F32)
        mix, copies = mixing_of(b, prior)
        mix_copies += copies
        folded = folded + (
            mix if b == 0 else jnp.dot(mix, advance, precision=HIGHEST, preferred_element_type=F32)
        )
        advance = eye + folded - jnp.sum(folded, axis=0, keepdims=True) / members
    weight = eye + folded - jnp.sum(folded, axis=1, keepdims=True) / members

    pairs = members * members
    choose = jnp.where(iota((pairs, members), 0) // members == iota((pairs, members), 1), 1.0, 0.0).astype(F32)
    spreadw = jnp.dot(choose, weight, precision=HIGHEST, preferred_element_type=F32)
    spreadw = jnp.where(iota((pairs, members), 0) % members == iota((pairs, members), 1), spreadw, 0.0)
    wb[...] = jnp.broadcast_to(jnp.sum(spreadw, axis=1, keepdims=True), (pairs, wide)).reshape(members, members, wide)

    for copy in st_copies:
        copy.wait_recv()

    def apply(to, dst):
        def one(i, carry):
            w = wb[to * own + i]
            acc = [jnp.zeros((8, wide), F32)] * fields
            for m in range(members):
                scale = jnp.broadcast_to(w[m:m + 1, :], (8, wide))
                for f in range(fields):
                    acc[f] = acc[f] + scale * xg[m // own, m % own, f]
            for f in range(fields):
                dst[to if dst is og else me, i, f] = acc[f]
            return carry

        lax.fori_loop(0, own, one, 0)

    fin_copies = []
    for d in range(1, nmem):
        to = lax.rem(me + d, nmem)
        apply(to, og)
        copy = pltpu.make_async_remote_copy(
            src_ref=og.at[to], dst_ref=og_in.at[me], send_sem=fin_send.at[d], recv_sem=fin_recv.at[d],
            device_id={"mem": to}, device_id_type=MESH,
        )
        copy.start()
        fin_copies.append(copy)
    apply(me, og_in)
    for copy in fin_copies:
        copy.wait_recv()
    for k in range(nmem):
        r, c = k // across * 8, k % across * wide
        out_ref[:, :, r:r + 8, c:c + wide] = og_in[k]

    @pl.when(tile > 0)
    def _():
        for copy in down:
            copy.wait_send()

    @pl.when(tile < last)
    def _():
        for copy in up:
            copy.wait_send()

    for copy in loc_copies + pri_copies + st_copies + mix_copies + fin_copies:
        copy.wait_send()


def on_device(nmem, ndom, x, smooth, cross, obs_tile, place, field, obs_weights, values, variance, localization):
    own, fields, rows, cols = x.shape
    batches, nobs = place.shape
    cap = 2 * nobs // ndom
    members = own * nmem
    wide = rows * cols // (8 * nmem)
    line = field * rows + place // (cols - 1)
    column = place % (cols - 1)
    attrs = jnp.concatenate(
        [
            line[:, None].astype(F32),
            column[:, None].astype(F32),
            jnp.transpose(obs_weights, (0, 2, 1)),
            values[:, None],
            variance[:, None],
        ],
        axis=1,
    )
    vmem = pl.BlockSpec(memory_space=pltpu.VMEM)
    anywhere = pl.BlockSpec(memory_space=pl.ANY)
    dma = pltpu.SemaphoreType.DMA
    return pl.pallas_call(
        functools.partial(kernel, nmem, ndom, cap),
        out_shape=jax.ShapeDtypeStruct(x.shape, F32),
        in_specs=[anywhere, anywhere, pl.BlockSpec(memory_space=pltpu.SMEM), vmem, vmem, vmem],
        out_specs=vmem,
        scratch_shapes=[
            pltpu.VMEM((own, fields, rows + 2 * HALO, cols), F32),
            pltpu.VMEM((fields, rows + 2 * HALO, cols), F32),
            pltpu.VMEM((nmem, own, fields, 8, wide), F32),
            pltpu.VMEM((own, fields * rows, cols), BF16),
            pltpu.VMEM((own, fields * rows, cols), BF16),
            pltpu.VMEM((batches, nobs, cap), BF16),
            pltpu.VMEM((batches, 8, cap), F32),
            pltpu.VMEM((batches, 2, cols, cap), BF16),
            pltpu.VMEM((batches, 2, fields * rows, cap), F32),
            pltpu.VMEM((ndom, 1, batches * nobs), F32),
            pltpu.VMEM((ndom, batches * nobs), F32),
            pltpu.VMEM((batches, ndom, cap), F32),
            pltpu.VMEM((nmem, own, 1, batches * cap), F32),
            pltpu.VMEM((nmem, own, fields, 8, wide), F32),
            pltpu.VMEM((nmem, own, fields, 8, wide), F32),
            pltpu.VMEM((nmem, own, fields, 8, wide), F32),
            pltpu.VMEM((batches, ndom, members, 128), F32),
            pltpu.VMEM((batches, ndom, members, 128), F32),
            pltpu.VMEM((members, members, wide), F32),
            dma((2,)), dma((4,)), dma((4,)),
            dma((ndom,)), dma((ndom,)),
            dma((nmem,)), dma((nmem,)),
            dma((nmem,)), dma((nmem,)),
            dma((batches, ndom)), dma((batches, ndom)),
            dma((nmem,)), dma((nmem,)),
        ],
        compiler_params=pltpu.CompilerParams(
            collective_id=0, has_side_effects=True, vmem_limit_bytes=48 * 1024 * 1024
        ),
    )(
        x,
        smooth,
        cross,
        obs_tile.reshape(batches * nobs // 128, 128),
        attrs,
        localization.reshape(1, batches * nobs),
    )


def solution(mesh):
    placed = (
        P("mem", None, "dom", None),
        P(None, "dom", None),
        P(),
        P(),
        P(),
        P(),
        P(),
        P(),
        P(),
        P(None, "dom", None),
    )
    return jax.shard_map(
        functools.partial(on_device, mesh.shape["mem"], mesh.shape["dom"]),
        mesh=mesh,
        in_specs=placed,
        out_specs=P("mem", None, "dom", None),
        check_vma=False,
    )
```

```python
import functools

import jax
import jax.numpy as jnp
from jax import lax
from jax.experimental import pallas as pl
from jax.experimental.pallas import tpu as pltpu
from jax.sharding import PartitionSpec as P

STEPS = 2
HALO = 8
GATHERED = 1
MESH = pl.DeviceIdType.MESH
HIGHEST = lax.Precision.HIGHEST
F32 = jnp.float32
BF16 = jnp.bfloat16


def three_parts(a):
    high = a.astype(BF16).astype(F32)
    rest = a - high
    middle = rest.astype(BF16).astype(F32)
    return jnp.concatenate([high, middle, rest - middle], axis=0).astype(BF16)


def two_parts(a):
    high = a.astype(BF16)
    return high, (a - high.astype(F32)).astype(BF16)


def partner(index, distance, count):
    to, step = 0, 1
    while step < count:
        bit = lax.rem(index // step, 2)
        to = to + step * (1 - bit if distance // step % 2 else bit)
        step *= 2
    return to


def iota(shape, dim):
    return lax.broadcasted_iota(jnp.int32, shape, dim)


def kernel(
    nmem, ndom, cap,
    x_ref, s_ref, c_ref, tile_hbm, place_hbm, field_hbm, weight_hbm, value_hbm, var_hbm, loc_hbm,
    out_ref,
    tile_ref, place_ref, field_ref, weight_ref, value_ref, var_ref, loc_ref,
    pad, spad, xs, xall, xu, xh, xl, pick, comp, csel, rsel, lbuf, lrow, lcomp,
    pbuf, xg, og, og_in, ps, rb, wb,
    local_sem, halo_send, halo_recv, loc_send, loc_recv, pri_send, pri_recv,
    st_send, st_recv, mix_send, mix_recv, fin_send, fin_recv,
):
    me = lax.axis_index("mem")
    tile = lax.axis_index("dom")
    own, fields, rows, cols = x_ref.shape
    members = own * nmem
    batches, nobs = place_ref.shape
    gathered = xs.shape[1]
    rest = fields - gathered
    groups = members // 8
    wide = xu.shape[-1]
    across = cols // wide
    lane_blocks = nobs // 128
    last = ndom - 1

    load_x = pltpu.make_async_copy(x_ref, pad.at[:, :, HALO:HALO + rows, :], local_sem.at[0])
    load_s = pltpu.make_async_copy(s_ref, spad.at[:, HALO:HALO + rows, :], local_sem.at[1])
    loads = [
        pltpu.make_async_copy(src, dst, local_sem.at[2 + i])
        for i, (src, dst) in enumerate([
            (tile_hbm, tile_ref), (place_hbm, place_ref), (field_hbm, field_ref), (weight_hbm, weight_ref),
            (value_hbm, value_ref), (var_hbm, var_ref), (loc_hbm, loc_ref),
        ])
    ]
    for copy in loads:
        copy.start()
    load_x.start()
    load_s.start()

    barrier = pltpu.get_barrier_semaphore()
    for d in range(1, nmem):
        pl.semaphore_signal(barrier, inc=1, device_id={"mem": lax.rem(me + d, nmem)}, device_id_type=MESH)
    for d in range(1, ndom):
        pl.semaphore_signal(barrier, inc=1, device_id={"dom": lax.rem(tile + d, ndom)}, device_id_type=MESH)

    @pl.when(tile == 0)
    def _():
        pad[:, :, 0:HALO, :] = jnp.zeros((own, fields, HALO, cols), F32)
        spad[:, 0:HALO, :] = jnp.zeros((fields, HALO, cols), F32)

    @pl.when(tile == last)
    def _():
        pad[:, :, HALO + rows:, :] = jnp.zeros((own, fields, HALO, cols), F32)
        spad[:, HALO + rows:, :] = jnp.zeros((fields, HALO, cols), F32)

    for copy in loads:
        copy.wait()

    count = batches * lane_blocks
    owned = tile_ref[...] == tile
    ownf = jnp.where(owned, 1.0, 0.0).astype(F32)
    ahead = jnp.where(iota((128, 128), 0) < iota((128, 128), 1), 1.0, 0.0).astype(BF16)
    row_i, row_j = iota((count, count), 0), iota((count, count), 1)
    prior_rows = jnp.where((row_j < row_i) & (row_j // lane_blocks == row_i // lane_blocks), 1.0, 0.0).astype(BF16)
    within = jnp.dot(ownf.astype(BF16), ahead, preferred_element_type=F32)
    offset = jnp.sum(jnp.dot(prior_rows, ownf.astype(BF16), preferred_element_type=F32), axis=1, keepdims=True)
    rank = jnp.where(owned, within + offset, -1.0)
    rank = jnp.concatenate([rank, jnp.full((128 - count, 128), -1.0, F32)], axis=0) if count < 128 else rank
    rank_t = jnp.transpose(rank)
    slots = iota((128, cap), 1).astype(F32)
    for b in range(batches):
        for k in range(lane_blocks):
            at = b * lane_blocks + k
            pick[b, k * 128:(k + 1) * 128, :] = jnp.where(rank_t[:, at:at + 1] == slots, 1.0, 0.0).astype(BF16)

    pl.semaphore_wait(barrier, nmem + ndom - 2)

    def halo(src, dst, to, slot):
        return pltpu.make_async_remote_copy(
            src_ref=src, dst_ref=dst, send_sem=halo_send.at[slot], recv_sem=halo_recv.at[slot],
            device_id={"dom": to}, device_id_type=MESH,
        )

    below = lax.rem(tile + ndom - 1, ndom)
    above = lax.rem(tile + 1, ndom)
    down = [
        halo(x_ref.at[:, :, 0:HALO, :], pad.at[:, :, HALO + rows:HALO + rows + HALO, :], below, 0),
        halo(s_ref.at[:, 0:HALO, :], spad.at[:, HALO + rows:HALO + rows + HALO, :], below, 1),
    ]
    up = [
        halo(x_ref.at[:, :, rows - HALO:rows, :], pad.at[:, :, 0:HALO, :], above, 2),
        halo(s_ref.at[:, rows - HALO:rows, :], spad.at[:, 0:HALO, :], above, 3),
    ]

    @pl.when(tile > 0)
    def _():
        for copy in down:
            copy.start()

    @pl.when(tile < last)
    def _():
        for copy in up:
            copy.start()


    for b in range(batches):
        place = place_ref[b:b + 1, :].astype(F32)
        row = jnp.floor((place + 0.5) * (1.0 / (cols - 1)))
        attrs = jnp.concatenate(
            [
                field_ref[b:b + 1, :].astype(F32) * rows + row,
                place - row * (cols - 1),
                weight_ref[b],
                value_ref[b:b + 1, :],
                var_ref[b:b + 1, :],
            ],
            axis=0,
        )
        got = jnp.dot(three_parts(attrs), pick[b], preferred_element_type=F32)
        packed = got[0:8] + got[8:16] + got[16:24]
        comp[b] = packed
        column = packed[1:2, :].astype(jnp.int32)
        line = packed[0:1, :].astype(jnp.int32)
        col_at = iota((cols, cap), 0)
        csel[b, 0] = jnp.where(col_at == column, 1.0, 0.0).astype(BF16)
        csel[b, 1] = jnp.where(col_at == column + 1, 1.0, 0.0).astype(BF16)
        line_at = iota((fields * rows, cap), 0)
        here, after = line_at == line, line_at == line + 1
        rsel[b, 0] = jnp.where(here, packed[2:3, :], jnp.where(after, packed[4:5, :], 0.0))
        rsel[b, 1] = jnp.where(here, packed[3:4, :], jnp.where(after, packed[5:6, :], 0.0))

    load_x.wait()
    load_s.wait()

    @pl.when(tile > 0)
    def _():
        for copy in up:
            copy.wait_recv()

    @pl.when(tile < last)
    def _():
        for copy in down:
            copy.wait_recv()

    loc_copies = []
    for d in range(ndom - 1, 0, -1):
        copy = pltpu.make_async_remote_copy(
            src_ref=loc_ref, dst_ref=lbuf.at[tile], send_sem=loc_send.at[d], recv_sem=loc_recv.at[d],
            device_id={"dom": partner(tile, d, ndom)}, device_id_type=MESH,
        )
        copy.start()
        loc_copies.append(copy)
    lbuf[tile] = loc_ref[...]

    height = rows + 2 * HALO
    lane = iota((height, cols), 1)

    def member(m, carry):
        x = [pad[m, f] for f in range(fields)]
        for _ in range(STEPS):
            new = []
            for f in range(fields):
                v = x[f]
                lap = pltpu.roll(v, 1, 0) + pltpu.roll(v, height - 1, 0)
                lap = lap + jnp.where(lane < cols - 1, pltpu.roll(v, cols - 1, 1), 0.0)
                lap = lap + jnp.where(lane > 0, pltpu.roll(v, 1, 1), 0.0) - 4.0 * v
                mixed = c_ref[f, 0] * x[0]
                for g in range(1, fields):
                    mixed = mixed + c_ref[f, g] * x[g]
                new.append(v + spad[f] * lap + mixed)
            x = new
        for f in range(fields):
            v = x[f][HALO:HALO + rows]
            xh[m, f * rows:(f + 1) * rows, :], xl[m, f * rows:(f + 1) * rows, :] = two_parts(v)
            if f < gathered:
                xs[m, f] = v
            else:
                for k in range(nmem):
                    r, c = k // across * 8, k % across * wide
                    xu[k, m, f - gathered] = v[r:r + 8, c:c + wide]
        return carry

    lax.fori_loop(0, own, member, 0)

    high = xh[...].reshape(own * fields * rows, cols)
    low = xl[...].reshape(own * fields * rows, cols)
    for b in range(batches):
        total = 0.0
        for side in range(2):
            t = jnp.dot(high, csel[b, side], preferred_element_type=F32)
            t = t + jnp.dot(low, csel[b, side], preferred_element_type=F32)
            total = total + jnp.sum(t.reshape(own, fields * rows, cap) * rsel[b, side], axis=1)
        for m in range(own):
            pbuf[me, m, :, b * cap:(b + 1) * cap] = total[m:m + 1]

    pri_copies = []
    for d in range(nmem - 1, 0, -1):
        copy = pltpu.make_async_remote_copy(
            src_ref=pbuf.at[me], dst_ref=pbuf.at[me], send_sem=pri_send.at[d], recv_sem=pri_recv.at[d],
            device_id={"mem": partner(me, d, nmem)}, device_id_type=MESH,
        )
        copy.start()
        pri_copies.append(copy)
    st_copies = []
    for d in range(nmem - 1, 0, -1):
        to = partner(me, d, nmem)
        for slot, (src, dst) in enumerate([(xu.at[to], xg.at[me]), (xs, xall.at[me])]):
            copy = pltpu.make_async_remote_copy(
                src_ref=src, dst_ref=dst, send_sem=st_send.at[slot, d], recv_sem=st_recv.at[slot, d],
                device_id={"mem": to}, device_id_type=MESH,
            )
            copy.start()
            st_copies.append(copy)
    xall[me] = xs[...]
    xg[me] = xu[me]

    for copy in loc_copies:
        copy.wait_recv()
    for t in range(ndom):
        lrow[t:t + 1, :] = lbuf[t]
    for b in range(batches):
        got = jnp.dot(
            three_parts(lrow[:, b * nobs:(b + 1) * nobs]), pick[b], preferred_element_type=F32
        )
        lcomp[b] = got[0:ndom] + got[ndom:2 * ndom] + got[2 * ndom:3 * ndom]

    for copy in pri_copies:
        copy.wait_recv()

    def gather_prior(b):
        return jnp.concatenate(
            [pbuf[i, m, :, b * cap:(b + 1) * cap] for i in range(nmem) for m in range(own)], axis=0
        )

    def mixing_of(b, prior):
        value = comp[b, 6:7, :]
        error = comp[b, 7:8, :]
        error = jnp.where(error > 0.0, error, 1.0)
        mean = jnp.sum(prior, axis=0, keepdims=True) / members
        spread = prior - mean
        total = jnp.sum(spread * spread, axis=0, keepdims=True) / (members - 1) + error
        root = jnp.sqrt(total)
        gain = (value - mean) / total - spread / (root * (jnp.sqrt(error) + root))
        left, right = [], []
        for g in range(groups):
            local = jnp.concatenate(
                [gain[8 * g:8 * g + 8] * lcomp[b, t:t + 1, :] for t in range(ndom)], axis=0
            )
            placed = [jnp.zeros((g * members, cap), F32)] if g else []
            placed += [spread / (members - 1)]
            placed += [jnp.zeros((128 - (g + 1) * members, cap), F32)] if (g + 1) * members < 128 else []
            local_high, local_low = two_parts(local)
            placed_high, placed_low = two_parts(jnp.concatenate(placed, axis=0))
            left += [local_high, local_high, local_low]
            right += [placed_high, placed_low, placed_high]
        part = lax.dot_general(
            jnp.concatenate(left, axis=1), jnp.concatenate(right, axis=1), (((1,), (1,)), ((), ())),
            preferred_element_type=F32,
        )
        for t in range(ndom):
            ps[b, t] = part[8 * t:8 * t + 8]
        copies = []
        for d in range(ndom - 1, 0, -1):
            to = partner(tile, d, ndom)
            copy = pltpu.make_async_remote_copy(
                src_ref=ps.at[b, to], dst_ref=rb.at[b, tile],
                send_sem=mix_send.at[b, d], recv_sem=mix_recv.at[b, d],
                device_id={"dom": to}, device_id_type=MESH,
            )
            copy.start()
            copies.append(copy)
        rb[b, tile] = ps[b, tile]
        for copy in copies:
            copy.wait_recv()
        got = jnp.sum(rb[b], axis=0)
        return jnp.concatenate([got[:, g * members:(g + 1) * members] for g in range(groups)], axis=0), copies

    eye = jnp.where(iota((members, members), 0) == iota((members, members), 1), 1.0, 0.0).astype(F32)
    mix_copies = []
    advance = eye
    folded = jnp.zeros((members, members), F32)
    for b in range(batches):
        prior = gather_prior(b)
        if b > 0:
            anomaly = prior - jnp.sum(prior, axis=0, keepdims=True) / members
            prior = prior + jnp.dot(folded, anomaly, precision=HIGHEST, preferred_element_type=F32)
        mix, copies = mixing_of(b, prior)
        mix_copies += copies
        folded = folded + (
            mix if b == 0 else jnp.dot(mix, advance, precision=HIGHEST, preferred_element_type=F32)
        )
        advance = eye + folded - jnp.sum(folded, axis=0, keepdims=True) / members
    weight = eye + folded - jnp.sum(folded, axis=1, keepdims=True) / members

    pairs = members * members
    choose = jnp.where(iota((pairs, members), 0) // members == iota((pairs, members), 1), 1.0, 0.0).astype(F32)
    spreadw = jnp.dot(choose, weight, precision=HIGHEST, preferred_element_type=F32)
    spreadw = jnp.where(iota((pairs, members), 0) % members == iota((pairs, members), 1), spreadw, 0.0)
    wb[...] = jnp.broadcast_to(jnp.sum(spreadw, axis=1, keepdims=True), (pairs, cols)).reshape(members, members, cols)

    for copy in st_copies:
        copy.wait_recv()

    def apply(to, dst):
        def one(i, carry):
            w = wb[to * own + i]
            acc = [jnp.zeros((8, wide), F32)] * rest
            for m in range(members):
                scale = jnp.broadcast_to(w[m:m + 1, 0:wide], (8, wide))
                for f in range(rest):
                    acc[f] = acc[f] + scale * xg[m // own, m % own, f]
            for f in range(rest):
                dst[to if dst is og else me, i, f] = acc[f]
            return carry

        lax.fori_loop(0, own, one, 0)

    fin_copies = []
    for d in range(nmem - 1, 0, -1):
        to = partner(me, d, nmem)
        apply(to, og)
        copy = pltpu.make_async_remote_copy(
            src_ref=og.at[to], dst_ref=og_in.at[me], send_sem=fin_send.at[d], recv_sem=fin_recv.at[d],
            device_id={"mem": to}, device_id_type=MESH,
        )
        copy.start()
        fin_copies.append(copy)
    apply(me, og_in)

    def apply_gathered(i, carry):
        w = wb[me * own + i]
        for f in range(gathered):
            acc = jnp.zeros((rows, cols), F32)
            for m in range(members):
                acc = acc + jnp.broadcast_to(w[m:m + 1, :], (rows, cols)) * xall[m // own, m % own, f]
            out_ref[i, f] = acc
        return carry

    lax.fori_loop(0, own, apply_gathered, 0)
    for copy in fin_copies:
        copy.wait_recv()
    for k in range(nmem):
        r, c = k // across * 8, k % across * wide
        out_ref[:, gathered:, r:r + 8, c:c + wide] = og_in[k]

    @pl.when(tile > 0)
    def _():
        for copy in down:
            copy.wait_send()

    @pl.when(tile < last)
    def _():
        for copy in up:
            copy.wait_send()

    for copy in loc_copies + pri_copies + st_copies + mix_copies + fin_copies:
        copy.wait_send()


def on_device(nmem, ndom, x, smooth, cross, obs_tile, place, field, obs_weights, values, variance, localization):
    own, fields, rows, cols = x.shape
    batches, nobs = place.shape
    cap = 2 * nobs // ndom
    members = own * nmem
    wide = rows * cols // (8 * nmem)
    rest = fields - GATHERED
    vmem = pl.BlockSpec(memory_space=pltpu.VMEM)
    anywhere = pl.BlockSpec(memory_space=pl.ANY)
    dma = pltpu.SemaphoreType.DMA
    return pl.pallas_call(
        functools.partial(kernel, nmem, ndom, cap),
        out_shape=jax.ShapeDtypeStruct(x.shape, F32),
        in_specs=[anywhere, anywhere, pl.BlockSpec(memory_space=pltpu.SMEM)] + [anywhere] * 7,
        out_specs=vmem,
        scratch_shapes=[
            pltpu.VMEM((batches * nobs // 128, 128), jnp.int32),
            pltpu.VMEM((batches, nobs), jnp.int32),
            pltpu.VMEM((batches, nobs), jnp.int32),
            pltpu.VMEM((batches, 4, nobs), F32),
            pltpu.VMEM((batches, nobs), F32),
            pltpu.VMEM((batches, nobs), F32),
            pltpu.VMEM((1, batches * nobs), F32),
            pltpu.VMEM((own, fields, rows + 2 * HALO, cols), F32),
            pltpu.VMEM((fields, rows + 2 * HALO, cols), F32),
            pltpu.VMEM((own, GATHERED, rows, cols), F32),
            pltpu.VMEM((nmem, own, GATHERED, rows, cols), F32),
            pltpu.VMEM((nmem, own, rest, 8, wide), F32),
            pltpu.VMEM((own, fields * rows, cols), BF16),
            pltpu.VMEM((own, fields * rows, cols), BF16),
            pltpu.VMEM((batches, nobs, cap), BF16),
            pltpu.VMEM((batches, 8, cap), F32),
            pltpu.VMEM((batches, 2, cols, cap), BF16),
            pltpu.VMEM((batches, 2, fields * rows, cap), F32),
            pltpu.VMEM((ndom, 1, batches * nobs), F32),
            pltpu.VMEM((ndom, batches * nobs), F32),
            pltpu.VMEM((batches, ndom, cap), F32),
            pltpu.VMEM((nmem, own, 1, batches * cap), F32),
            pltpu.VMEM((nmem, own, rest, 8, wide), F32),
            pltpu.VMEM((nmem, own, rest, 8, wide), F32),
            pltpu.VMEM((nmem, own, rest, 8, wide), F32),
            pltpu.VMEM((batches, ndom, 8, 128), F32),
            pltpu.VMEM((batches, ndom, 8, 128), F32),
            pltpu.VMEM((members, members, cols), F32),
            dma((9,)), dma((4,)), dma((4,)),
            dma((ndom,)), dma((ndom,)),
            dma((nmem,)), dma((nmem,)),
            dma((2, nmem)), dma((2, nmem)),
            dma((batches, ndom)), dma((batches, ndom)),
            dma((nmem,)), dma((nmem,)),
        ],
        compiler_params=pltpu.CompilerParams(
            collective_id=0, has_side_effects=True, vmem_limit_bytes=60 * 1024 * 1024
        ),
    )(
        x,
        smooth,
        cross,
        obs_tile.reshape(batches * nobs // 128, 128),
        place,
        field,
        jnp.transpose(obs_weights, (0, 2, 1)),
        values,
        variance,
        localization.reshape(1, batches * nobs),
    )


def solution(mesh):
    placed = (
        P("mem", None, "dom", None),
        P(None, "dom", None),
        P(),
        P(),
        P(),
        P(),
        P(),
        P(),
        P(),
        P(None, "dom", None),
    )
    return jax.shard_map(
        functools.partial(on_device, mesh.shape["mem"], mesh.shape["dom"]),
        mesh=mesh,
        in_specs=placed,
        out_specs=P("mem", None, "dom", None),
        check_vma=False,
    )
```

```python
import functools

import jax
import jax.numpy as jnp
from jax import lax
from jax.experimental import pallas as pl
from jax.experimental.pallas import tpu as pltpu
from jax.sharding import PartitionSpec as P

STEPS = 2
HALO = 8
GATHERED = 1
MESH = pl.DeviceIdType.MESH
HIGHEST = lax.Precision.HIGHEST
F32 = jnp.float32
BF16 = jnp.bfloat16


def three_parts(a):
    high = a.astype(BF16).astype(F32)
    rest = a - high
    middle = rest.astype(BF16).astype(F32)
    return jnp.concatenate([high, middle, rest - middle], axis=0).astype(BF16)


def two_parts(a):
    high = a.astype(BF16)
    return high, (a - high.astype(F32)).astype(BF16)


def partner(index, distance, count):
    to, step = 0, 1
    while step < count:
        bit = lax.rem(index // step, 2)
        to = to + step * (1 - bit if distance // step % 2 else bit)
        step *= 2
    return to


def iota(shape, dim):
    return lax.broadcasted_iota(jnp.int32, shape, dim)


def kernel(
    nmem, ndom, cap,
    x_ref, s_ref, c_ref, tile_hbm, place_hbm, field_hbm, weight_hbm, value_hbm, var_hbm, loc_hbm,
    out_ref,
    tile_ref, place_ref, field_ref, weight_ref, value_ref, var_ref, loc_ref,
    pad, spad, xs, xall, xu, xh, xl, pick, comp, csel, rsel, lbuf, lrow, lcomp,
    pbuf, xg, og, og_in, ps, rb, wb,
    local_sem, halo_send, halo_recv, loc_send, loc_recv, pri_send, pri_recv,
    st_send, st_recv, mix_send, mix_recv, fin_send, fin_recv,
):
    me = lax.axis_index("mem")
    tile = lax.axis_index("dom")
    own, fields, rows, cols = x_ref.shape
    members = own * nmem
    batches, nobs = place_ref.shape
    gathered = xs.shape[1]
    rest = fields - gathered
    groups = members // 8
    wide = xu.shape[-1]
    across = cols // wide
    lane_blocks = nobs // 128
    last = ndom - 1

    load_x = pltpu.make_async_copy(x_ref, pad.at[:, :, HALO:HALO + rows, :], local_sem.at[0])
    load_s = pltpu.make_async_copy(s_ref, spad.at[:, HALO:HALO + rows, :], local_sem.at[1])
    loads = [
        pltpu.make_async_copy(src, dst, local_sem.at[2 + i])
        for i, (src, dst) in enumerate([
            (tile_hbm, tile_ref), (place_hbm, place_ref), (field_hbm, field_ref), (weight_hbm, weight_ref),
            (value_hbm, value_ref), (var_hbm, var_ref), (loc_hbm, loc_ref),
        ])
    ]
    for copy in loads:
        copy.start()
    load_x.start()
    load_s.start()

    barrier = pltpu.get_barrier_semaphore()
    for d in range(1, nmem):
        pl.semaphore_signal(barrier, inc=1, device_id={"mem": lax.rem(me + d, nmem)}, device_id_type=MESH)
    for d in range(1, ndom):
        pl.semaphore_signal(barrier, inc=1, device_id={"dom": lax.rem(tile + d, ndom)}, device_id_type=MESH)

    @pl.when(tile == 0)
    def _():
        pad[:, :, 0:HALO, :] = jnp.zeros((own, fields, HALO, cols), F32)
        spad[:, 0:HALO, :] = jnp.zeros((fields, HALO, cols), F32)

    @pl.when(tile == last)
    def _():
        pad[:, :, HALO + rows:, :] = jnp.zeros((own, fields, HALO, cols), F32)
        spad[:, HALO + rows:, :] = jnp.zeros((fields, HALO, cols), F32)

    pl.semaphore_wait(barrier, nmem + ndom - 2)

    def halo(src, dst, to, slot):
        return pltpu.make_async_remote_copy(
            src_ref=src, dst_ref=dst, send_sem=halo_send.at[slot], recv_sem=halo_recv.at[slot],
            device_id={"dom": to}, device_id_type=MESH,
        )

    below = lax.rem(tile + ndom - 1, ndom)
    above = lax.rem(tile + 1, ndom)
    down = [
        halo(x_ref.at[:, :, 0:HALO, :], pad.at[:, :, HALO + rows:HALO + rows + HALO, :], below, 0),
        halo(s_ref.at[:, 0:HALO, :], spad.at[:, HALO + rows:HALO + rows + HALO, :], below, 1),
    ]
    up = [
        halo(x_ref.at[:, :, rows - HALO:rows, :], pad.at[:, :, 0:HALO, :], above, 2),
        halo(s_ref.at[:, rows - HALO:rows, :], spad.at[:, 0:HALO, :], above, 3),
    ]

    @pl.when(tile > 0)
    def _():
        for copy in down:
            copy.start()

    @pl.when(tile < last)
    def _():
        for copy in up:
            copy.start()


    for copy in loads:
        copy.wait()

    count = batches * lane_blocks
    owned = tile_ref[...] == tile
    ownf = jnp.where(owned, 1.0, 0.0).astype(F32)
    ahead = jnp.where(iota((128, 128), 0) < iota((128, 128), 1), 1.0, 0.0).astype(BF16)
    row_i, row_j = iota((count, count), 0), iota((count, count), 1)
    prior_rows = jnp.where((row_j < row_i) & (row_j // lane_blocks == row_i // lane_blocks), 1.0, 0.0).astype(BF16)
    within = jnp.dot(ownf.astype(BF16), ahead, preferred_element_type=F32)
    offset = jnp.sum(jnp.dot(prior_rows, ownf.astype(BF16), preferred_element_type=F32), axis=1, keepdims=True)
    rank = jnp.where(owned, within + offset, -1.0)
    rank = jnp.concatenate([rank, jnp.full((128 - count, 128), -1.0, F32)], axis=0) if count < 128 else rank
    rank_t = jnp.transpose(rank)
    slots = iota((128, cap), 1).astype(F32)

    def prepare(b):
        for k in range(lane_blocks):
            at = b * lane_blocks + k
            pick[b, k * 128:(k + 1) * 128, :] = jnp.where(rank_t[:, at:at + 1] == slots, 1.0, 0.0).astype(BF16)
        place = place_ref[b:b + 1, :].astype(F32)
        row = jnp.floor((place + 0.5) * (1.0 / (cols - 1)))
        attrs = jnp.concatenate(
            [
                field_ref[b:b + 1, :].astype(F32) * rows + row,
                place - row * (cols - 1),
                weight_ref[b],
                value_ref[b:b + 1, :],
                var_ref[b:b + 1, :],
            ],
            axis=0,
        )
        got = jnp.dot(three_parts(attrs), pick[b], preferred_element_type=F32)
        packed = got[0:8] + got[8:16] + got[16:24]
        comp[b] = packed
        column = packed[1:2, :].astype(jnp.int32)
        line = packed[0:1, :].astype(jnp.int32)
        col_at = iota((cols, cap), 0)
        csel[b, 0] = jnp.where(col_at == column, 1.0, 0.0).astype(BF16)
        csel[b, 1] = jnp.where(col_at == column + 1, 1.0, 0.0).astype(BF16)
        line_at = iota((fields * rows, cap), 0)
        here, after = line_at == line, line_at == line + 1
        rsel[b, 0] = jnp.where(here, packed[2:3, :], jnp.where(after, packed[4:5, :], 0.0))
        rsel[b, 1] = jnp.where(here, packed[3:4, :], jnp.where(after, packed[5:6, :], 0.0))

    prepare(0)

    load_x.wait()
    load_s.wait()

    @pl.when(tile > 0)
    def _():
        for copy in up:
            copy.wait_recv()

    @pl.when(tile < last)
    def _():
        for copy in down:
            copy.wait_recv()

    loc_copies = []
    for d in range(ndom - 1, 0, -1):
        copy = pltpu.make_async_remote_copy(
            src_ref=loc_ref, dst_ref=lbuf.at[tile], send_sem=loc_send.at[d], recv_sem=loc_recv.at[d],
            device_id={"dom": partner(tile, d, ndom)}, device_id_type=MESH,
        )
        copy.start()
        loc_copies.append(copy)
    lbuf[tile] = loc_ref[...]

    height = rows + 2 * HALO
    lane = iota((height, cols), 1)

    def member(m, carry):
        x = [pad[m, f] for f in range(fields)]
        for _ in range(STEPS):
            new = []
            for f in range(fields):
                v = x[f]
                lap = pltpu.roll(v, 1, 0) + pltpu.roll(v, height - 1, 0)
                lap = lap + jnp.where(lane < cols - 1, pltpu.roll(v, cols - 1, 1), 0.0)
                lap = lap + jnp.where(lane > 0, pltpu.roll(v, 1, 1), 0.0) - 4.0 * v
                mixed = c_ref[f, 0] * x[0]
                for g in range(1, fields):
                    mixed = mixed + c_ref[f, g] * x[g]
                new.append(v + spad[f] * lap + mixed)
            x = new
        for f in range(fields):
            v = x[f][HALO:HALO + rows]
            xh[m, f * rows:(f + 1) * rows, :], xl[m, f * rows:(f + 1) * rows, :] = two_parts(v)
            if f < gathered:
                xs[m, f] = v
            else:
                for k in range(nmem):
                    r, c = k // across * 8, k % across * wide
                    xu[k, m, f - gathered] = v[r:r + 8, c:c + wide]
        return carry

    lax.fori_loop(0, own, member, 0)

    pri_copies, st_copies = [], []

    def observe(b):
        high = xh[...].reshape(own * fields * rows, cols)
        low = xl[...].reshape(own * fields * rows, cols)
        total = 0.0
        for side in range(2):
            t = jnp.dot(high, csel[b, side], preferred_element_type=F32)
            t = t + jnp.dot(low, csel[b, side], preferred_element_type=F32)
            total = total + jnp.sum(t.reshape(own, fields * rows, cap) * rsel[b, side], axis=1)
        for m in range(own):
            pbuf[b, me, m] = total[m:m + 1]
        copies = []
        for d in range(nmem - 1, 0, -1):
            copy = pltpu.make_async_remote_copy(
                src_ref=pbuf.at[b, me], dst_ref=pbuf.at[b, me],
                send_sem=pri_send.at[b, d], recv_sem=pri_recv.at[b, d],
                device_id={"mem": partner(me, d, nmem)}, device_id_type=MESH,
            )
            copy.start()
            copies.append(copy)
        pri_copies.append(copies)

    def send_states(slot):
        for d in range(nmem - 1, 0, -1):
            to = partner(me, d, nmem)
            src, dst = [(xu.at[to], xg.at[me]), (xs, xall.at[me])][slot]
            copy = pltpu.make_async_remote_copy(
                src_ref=src, dst_ref=dst, send_sem=st_send.at[slot, d], recv_sem=st_recv.at[slot, d],
                device_id={"mem": to}, device_id_type=MESH,
            )
            copy.start()
            st_copies.append(copy)

    def localize(b):
        got = jnp.dot(
            three_parts(lrow[:, b * nobs:(b + 1) * nobs]), pick[b], preferred_element_type=F32
        )
        lcomp[b] = got[0:ndom] + got[ndom:2 * ndom] + got[2 * ndom:3 * ndom]

    def gather_prior(b):
        for copy in pri_copies[b]:
            copy.wait_recv()
        return jnp.concatenate([pbuf[b, i, m] for i in range(nmem) for m in range(own)], axis=0)

    observe(0)
    send_states(0)
    xg[me] = xu[me]

    for copy in loc_copies:
        copy.wait_recv()
    for t in range(ndom):
        lrow[t:t + 1, :] = lbuf[t]
    localize(0)
    for b in range(1, batches):
        prepare(b)

    def mixing_of(b, prior):
        value = comp[b, 6:7, :]
        error = comp[b, 7:8, :]
        error = jnp.where(error > 0.0, error, 1.0)
        mean = jnp.sum(prior, axis=0, keepdims=True) / members
        spread = prior - mean
        total = jnp.sum(spread * spread, axis=0, keepdims=True) / (members - 1) + error
        root = jnp.sqrt(total)
        gain = (value - mean) / total - spread / (root * (jnp.sqrt(error) + root))
        left, right = [], []
        for g in range(groups):
            local = jnp.concatenate(
                [gain[8 * g:8 * g + 8] * lcomp[b, t:t + 1, :] for t in range(ndom)], axis=0
            )
            placed = [jnp.zeros((g * members, cap), F32)] if g else []
            placed += [spread / (members - 1)]
            placed += [jnp.zeros((128 - (g + 1) * members, cap), F32)] if (g + 1) * members < 128 else []
            local_high, local_low = two_parts(local)
            placed_high, placed_low = two_parts(jnp.concatenate(placed, axis=0))
            left += [local_high, local_high, local_low]
            right += [placed_high, placed_low, placed_high]
        part = lax.dot_general(
            jnp.concatenate(left, axis=1), jnp.concatenate(right, axis=1), (((1,), (1,)), ((), ())),
            preferred_element_type=F32,
        )
        for t in range(ndom):
            ps[b, t] = part[8 * t:8 * t + 8]
        copies = []
        for d in range(ndom - 1, 0, -1):
            to = partner(tile, d, ndom)
            copy = pltpu.make_async_remote_copy(
                src_ref=ps.at[b, to], dst_ref=rb.at[b, tile],
                send_sem=mix_send.at[b, d], recv_sem=mix_recv.at[b, d],
                device_id={"dom": to}, device_id_type=MESH,
            )
            copy.start()
            copies.append(copy)
        rb[b, tile] = ps[b, tile]
        return copies

    def received(b, copies):
        for copy in copies:
            copy.wait_recv()
        got = jnp.sum(rb[b], axis=0)
        return jnp.concatenate([got[:, g * members:(g + 1) * members] for g in range(groups)], axis=0)

    eye = jnp.where(iota((members, members), 0) == iota((members, members), 1), 1.0, 0.0).astype(F32)
    mix_copies = []
    advance = eye
    folded = jnp.zeros((members, members), F32)
    for b in range(batches):
        prior = gather_prior(b)
        if b > 0:
            anomaly = prior - jnp.sum(prior, axis=0, keepdims=True) / members
            prior = prior + jnp.dot(folded, anomaly, precision=HIGHEST, preferred_element_type=F32)
        copies = mixing_of(b, prior)
        mix_copies += copies
        if b == 0:
            for later in range(1, batches):
                observe(later)
            send_states(1)
            xall[me] = xs[...]
            for later in range(1, batches):
                localize(later)
        mix = received(b, copies)
        folded = folded + (
            mix if b == 0 else jnp.dot(mix, advance, precision=HIGHEST, preferred_element_type=F32)
        )
        advance = eye + folded - jnp.sum(folded, axis=0, keepdims=True) / members
    weight = eye + folded - jnp.sum(folded, axis=1, keepdims=True) / members

    pairs = members * members
    choose = jnp.where(iota((pairs, members), 0) // members == iota((pairs, members), 1), 1.0, 0.0).astype(F32)
    spreadw = jnp.dot(choose, weight, precision=HIGHEST, preferred_element_type=F32)
    spreadw = jnp.where(iota((pairs, members), 0) % members == iota((pairs, members), 1), spreadw, 0.0)
    wb[...] = jnp.broadcast_to(jnp.sum(spreadw, axis=1, keepdims=True), (pairs, cols)).reshape(members, members, cols)

    for copy in st_copies[0:nmem - 1]:
        copy.wait_recv()

    def apply(to, dst):
        def one(i, carry):
            w = wb[to * own + i]
            acc = [jnp.zeros((8, wide), F32)] * rest
            for m in range(members):
                scale = jnp.broadcast_to(w[m:m + 1, 0:wide], (8, wide))
                for f in range(rest):
                    acc[f] = acc[f] + scale * xg[m // own, m % own, f]
            for f in range(rest):
                dst[to if dst is og else me, i, f] = acc[f]
            return carry

        lax.fori_loop(0, own, one, 0)

    fin_copies = []
    for d in range(nmem - 1, 0, -1):
        to = partner(me, d, nmem)
        apply(to, og)
        copy = pltpu.make_async_remote_copy(
            src_ref=og.at[to], dst_ref=og_in.at[me], send_sem=fin_send.at[d], recv_sem=fin_recv.at[d],
            device_id={"mem": to}, device_id_type=MESH,
        )
        copy.start()
        fin_copies.append(copy)
    apply(me, og_in)

    for copy in st_copies[nmem - 1:]:
        copy.wait_recv()

    def apply_gathered(i, carry):
        w = wb[me * own + i]
        for f in range(gathered):
            acc = jnp.zeros((rows, cols), F32)
            for m in range(members):
                acc = acc + jnp.broadcast_to(w[m:m + 1, :], (rows, cols)) * xall[m // own, m % own, f]
            out_ref[i, f] = acc
        return carry

    lax.fori_loop(0, own, apply_gathered, 0)
    for copy in fin_copies:
        copy.wait_recv()
    for k in range(nmem):
        r, c = k // across * 8, k % across * wide
        out_ref[:, gathered:, r:r + 8, c:c + wide] = og_in[k]

    @pl.when(tile > 0)
    def _():
        for copy in down:
            copy.wait_send()

    @pl.when(tile < last)
    def _():
        for copy in up:
            copy.wait_send()

    for copy in loc_copies + sum(pri_copies, []) + st_copies + mix_copies + fin_copies:
        copy.wait_send()


def on_device(nmem, ndom, x, smooth, cross, obs_tile, place, field, obs_weights, values, variance, localization):
    own, fields, rows, cols = x.shape
    batches, nobs = place.shape
    cap = 2 * nobs // ndom
    members = own * nmem
    wide = rows * cols // (8 * nmem)
    rest = fields - GATHERED
    vmem = pl.BlockSpec(memory_space=pltpu.VMEM)
    anywhere = pl.BlockSpec(memory_space=pltpu.HBM)
    dma = pltpu.SemaphoreType.DMA
    return pl.pallas_call(
        functools.partial(kernel, nmem, ndom, cap),
        out_shape=jax.ShapeDtypeStruct(x.shape, F32),
        in_specs=[anywhere, anywhere, pl.BlockSpec(memory_space=pltpu.SMEM)] + [anywhere] * 7,
        out_specs=vmem,
        scratch_shapes=[
            pltpu.VMEM((batches * nobs // 128, 128), jnp.int32),
            pltpu.VMEM((batches, nobs), jnp.int32),
            pltpu.VMEM((batches, nobs), jnp.int32),
            pltpu.VMEM((batches, 4, nobs), F32),
            pltpu.VMEM((batches, nobs), F32),
            pltpu.VMEM((batches, nobs), F32),
            pltpu.VMEM((1, batches * nobs), F32),
            pltpu.VMEM((own, fields, rows + 2 * HALO, cols), F32),
            pltpu.VMEM((fields, rows + 2 * HALO, cols), F32),
            pltpu.VMEM((own, GATHERED, rows, cols), F32),
            pltpu.VMEM((nmem, own, GATHERED, rows, cols), F32),
            pltpu.VMEM((nmem, own, rest, 8, wide), F32),
            pltpu.VMEM((own, fields * rows, cols), BF16),
            pltpu.VMEM((own, fields * rows, cols), BF16),
            pltpu.VMEM((batches, nobs, cap), BF16),
            pltpu.VMEM((batches, 8, cap), F32),
            pltpu.VMEM((batches, 2, cols, cap), BF16),
            pltpu.VMEM((batches, 2, fields * rows, cap), F32),
            pltpu.VMEM((ndom, 1, batches * nobs), F32),
            pltpu.VMEM((ndom, batches * nobs), F32),
            pltpu.VMEM((batches, ndom, cap), F32),
            pltpu.VMEM((batches, nmem, own, 1, cap), F32),
            pltpu.VMEM((nmem, own, rest, 8, wide), F32),
            pltpu.VMEM((nmem, own, rest, 8, wide), F32),
            pltpu.VMEM((nmem, own, rest, 8, wide), F32),
            pltpu.VMEM((batches, ndom, 8, 128), F32),
            pltpu.VMEM((batches, ndom, 8, 128), F32),
            pltpu.VMEM((members, members, cols), F32),
            dma((9,)), dma((4,)), dma((4,)),
            dma((ndom,)), dma((ndom,)),
            dma((batches, nmem)), dma((batches, nmem)),
            dma((2, nmem)), dma((2, nmem)),
            dma((batches, ndom)), dma((batches, ndom)),
            dma((nmem,)), dma((nmem,)),
        ],
        compiler_params=pltpu.CompilerParams(
            collective_id=0, has_side_effects=True, vmem_limit_bytes=60 * 1024 * 1024
        ),
    )(
        x,
        smooth,
        cross,
        obs_tile.reshape(batches * nobs // 128, 128),
        place,
        field,
        jnp.transpose(obs_weights, (0, 2, 1)),
        values,
        variance,
        localization.reshape(1, batches * nobs),
    )


def solution(mesh):
    placed = (
        P("mem", None, "dom", None),
        P(None, "dom", None),
        P(),
        P(),
        P(),
        P(),
        P(),
        P(),
        P(),
        P(None, "dom", None),
    )
    return jax.shard_map(
        functools.partial(on_device, mesh.shape["mem"], mesh.shape["dom"]),
        mesh=mesh,
        in_specs=placed,
        out_specs=P("mem", None, "dom", None),
        check_vma=False,
    )
```

```python
import functools

import jax
import jax.numpy as jnp
from jax import lax
from jax.experimental import pallas as pl
from jax.experimental.pallas import tpu as pltpu
from jax.sharding import PartitionSpec as P

STEPS = 2
HALO = 8
GATHERED = 1
MESH = pl.DeviceIdType.MESH
HIGHEST = lax.Precision.HIGHEST
F32 = jnp.float32
BF16 = jnp.bfloat16


def three_parts(a):
    high = a.astype(BF16).astype(F32)
    rest = a - high
    middle = rest.astype(BF16).astype(F32)
    return jnp.concatenate([high, middle, rest - middle], axis=0).astype(BF16)


def two_parts(a):
    high = a.astype(BF16)
    return high, (a - high.astype(F32)).astype(BF16)


def partner(index, distance, count):
    to, step = 0, 1
    while step < count:
        bit = lax.rem(index // step, 2)
        to = to + step * (1 - bit if distance // step % 2 else bit)
        step *= 2
    return to


def iota(shape, dim):
    return lax.broadcasted_iota(jnp.int32, shape, dim)


def kernel(
    nmem, ndom, cap,
    x_ref, s_ref, c_ref, tile_hbm, place_hbm, field_hbm, weight_hbm, value_hbm, var_hbm, loc_hbm,
    out_ref,
    tile_ref, place_ref, field_ref, weight_ref, value_ref, var_ref, loc_ref,
    pad, spad, xs, xall, xu, xh, xl, pick, comp, csel, rsel, lbuf, lrow, lcomp,
    pbuf, xg, og, og_in, ps, rb, wb,
    local_sem, halo_send, halo_recv, loc_send, loc_recv, pri_send, pri_recv,
    st_send, st_recv, mix_send, mix_recv, fin_send, fin_recv,
):
    me = lax.axis_index("mem")
    tile = lax.axis_index("dom")
    own, fields, rows, cols = x_ref.shape
    members = own * nmem
    batches, nobs = place_ref.shape
    gathered = xs.shape[1]
    rest = fields - gathered
    groups = members // 8
    wide = xu.shape[-1]
    across = cols // wide
    lane_blocks = nobs // 128
    last = ndom - 1

    load_x = pltpu.make_async_copy(x_ref, pad.at[:, :, HALO:HALO + rows, :], local_sem.at[0])
    load_s = pltpu.make_async_copy(s_ref, spad.at[:, HALO:HALO + rows, :], local_sem.at[1])
    loads = [
        pltpu.make_async_copy(src, dst, local_sem.at[2 + i])
        for i, (src, dst) in enumerate([
            (tile_hbm, tile_ref), (place_hbm, place_ref), (field_hbm, field_ref), (weight_hbm, weight_ref),
            (value_hbm, value_ref), (var_hbm, var_ref), (loc_hbm, loc_ref),
        ])
    ]
    for copy in loads:
        copy.start()
    load_x.start()
    load_s.start()

    barrier = pltpu.get_barrier_semaphore()
    for d in range(1, nmem):
        pl.semaphore_signal(barrier, inc=1, device_id={"mem": lax.rem(me + d, nmem)}, device_id_type=MESH)
    for d in range(1, ndom):
        pl.semaphore_signal(barrier, inc=1, device_id={"dom": lax.rem(tile + d, ndom)}, device_id_type=MESH)

    @pl.when(tile == 0)
    def _():
        pad[:, :, 0:HALO, :] = jnp.zeros((own, fields, HALO, cols), F32)
        spad[:, 0:HALO, :] = jnp.zeros((fields, HALO, cols), F32)

    @pl.when(tile == last)
    def _():
        pad[:, :, HALO + rows:, :] = jnp.zeros((own, fields, HALO, cols), F32)
        spad[:, HALO + rows:, :] = jnp.zeros((fields, HALO, cols), F32)

    pl.semaphore_wait(barrier, nmem + ndom - 2)

    def halo(src, dst, to, slot):
        return pltpu.make_async_remote_copy(
            src_ref=src, dst_ref=dst, send_sem=halo_send.at[slot], recv_sem=halo_recv.at[slot],
            device_id={"dom": to}, device_id_type=MESH,
        )

    below = lax.rem(tile + ndom - 1, ndom)
    above = lax.rem(tile + 1, ndom)
    down = [
        halo(x_ref.at[:, :, 0:HALO, :], pad.at[:, :, HALO + rows:HALO + rows + HALO, :], below, 0),
        halo(s_ref.at[:, 0:HALO, :], spad.at[:, HALO + rows:HALO + rows + HALO, :], below, 1),
    ]
    up = [
        halo(x_ref.at[:, :, rows - HALO:rows, :], pad.at[:, :, 0:HALO, :], above, 2),
        halo(s_ref.at[:, rows - HALO:rows, :], spad.at[:, 0:HALO, :], above, 3),
    ]

    @pl.when(tile > 0)
    def _():
        for copy in down:
            copy.start()

    @pl.when(tile < last)
    def _():
        for copy in up:
            copy.start()


    for copy in loads:
        copy.wait()

    count = batches * lane_blocks
    owned = tile_ref[...] == tile
    ownf = jnp.where(owned, 1.0, 0.0).astype(F32)
    ahead = jnp.where(iota((128, 128), 0) < iota((128, 128), 1), 1.0, 0.0).astype(BF16)
    row_i, row_j = iota((count, count), 0), iota((count, count), 1)
    prior_rows = jnp.where((row_j < row_i) & (row_j // lane_blocks == row_i // lane_blocks), 1.0, 0.0).astype(BF16)
    within = jnp.dot(ownf.astype(BF16), ahead, preferred_element_type=F32)
    offset = jnp.sum(jnp.dot(prior_rows, ownf.astype(BF16), preferred_element_type=F32), axis=1, keepdims=True)
    rank = jnp.where(owned, within + offset, -1.0)
    rank = jnp.concatenate([rank, jnp.full((128 - count, 128), -1.0, F32)], axis=0) if count < 128 else rank
    rank_t = jnp.transpose(rank)
    slots = iota((128, cap), 1).astype(F32)

    def prepare(b):
        for k in range(lane_blocks):
            at = b * lane_blocks + k
            pick[b, k * 128:(k + 1) * 128, :] = jnp.where(rank_t[:, at:at + 1] == slots, 1.0, 0.0).astype(BF16)
        place = place_ref[b:b + 1, :].astype(F32)
        row = jnp.floor((place + 0.5) * (1.0 / (cols - 1)))
        attrs = jnp.concatenate(
            [
                field_ref[b:b + 1, :].astype(F32) * rows + row,
                place - row * (cols - 1),
                weight_ref[b],
                value_ref[b:b + 1, :],
                var_ref[b:b + 1, :],
            ],
            axis=0,
        )
        got = jnp.dot(three_parts(attrs), pick[b], preferred_element_type=F32)
        packed = got[0:8] + got[8:16] + got[16:24]
        comp[b] = packed
        column = packed[1:2, :].astype(jnp.int32)
        line = packed[0:1, :].astype(jnp.int32)
        col_at = iota((cols, cap), 0)
        csel[b, 0] = jnp.where(col_at == column, 1.0, 0.0).astype(BF16)
        csel[b, 1] = jnp.where(col_at == column + 1, 1.0, 0.0).astype(BF16)
        line_at = iota((fields * rows, cap), 0)
        here, after = line_at == line, line_at == line + 1
        rsel[b, 0] = jnp.where(here, packed[2:3, :], jnp.where(after, packed[4:5, :], 0.0))
        rsel[b, 1] = jnp.where(here, packed[3:4, :], jnp.where(after, packed[5:6, :], 0.0))

    prepare(0)

    load_x.wait()
    load_s.wait()

    @pl.when(tile > 0)
    def _():
        for copy in up:
            copy.wait_recv()

    @pl.when(tile < last)
    def _():
        for copy in down:
            copy.wait_recv()

    loc_copies = []
    for d in range(ndom - 1, 0, -1):
        copy = pltpu.make_async_remote_copy(
            src_ref=loc_ref, dst_ref=lbuf.at[tile], send_sem=loc_send.at[d], recv_sem=loc_recv.at[d],
            device_id={"dom": partner(tile, d, ndom)}, device_id_type=MESH,
        )
        copy.start()
        loc_copies.append(copy)
    lbuf[tile] = loc_ref[...]

    height = rows + 2 * HALO
    lane = iota((height, cols), 1)

    def member(m, carry):
        x = [pad[m, f] for f in range(fields)]
        for _ in range(STEPS):
            new = []
            for f in range(fields):
                v = x[f]
                lap = pltpu.roll(v, 1, 0) + pltpu.roll(v, height - 1, 0)
                lap = lap + jnp.where(lane < cols - 1, pltpu.roll(v, cols - 1, 1), 0.0)
                lap = lap + jnp.where(lane > 0, pltpu.roll(v, 1, 1), 0.0) - 4.0 * v
                mixed = c_ref[f, 0] * x[0]
                for g in range(1, fields):
                    mixed = mixed + c_ref[f, g] * x[g]
                new.append(v + spad[f] * lap + mixed)
            x = new
        for f in range(fields):
            v = x[f][HALO:HALO + rows]
            xh[m, f * rows:(f + 1) * rows, :], xl[m, f * rows:(f + 1) * rows, :] = two_parts(v)
            if f < gathered:
                xs[m, f] = v
            else:
                for k in range(nmem):
                    r, c = k // across * 8, k % across * wide
                    xu[k, m, f - gathered] = v[r:r + 8, c:c + wide]
        return carry

    lax.fori_loop(0, own, member, 0)

    pri_copies, st_copies = [], []

    def observe(b):
        high = xh[...].reshape(own * fields * rows, cols)
        low = xl[...].reshape(own * fields * rows, cols)
        total = 0.0
        for side in range(2):
            t = jnp.dot(high, csel[b, side], preferred_element_type=F32)
            t = t + jnp.dot(low, csel[b, side], preferred_element_type=F32)
            total = total + jnp.sum(t.reshape(own, fields * rows, cap) * rsel[b, side], axis=1)
        for m in range(own):
            pbuf[b, me, m] = total[m:m + 1]
        copies = []
        for d in range(nmem - 1, 0, -1):
            copy = pltpu.make_async_remote_copy(
                src_ref=pbuf.at[b, me], dst_ref=pbuf.at[b, me],
                send_sem=pri_send.at[b, d], recv_sem=pri_recv.at[b, d],
                device_id={"mem": partner(me, d, nmem)}, device_id_type=MESH,
            )
            copy.start()
            copies.append(copy)
        pri_copies.append(copies)

    def send_states(slot):
        for d in range(nmem - 1, 0, -1):
            to = partner(me, d, nmem)
            src, dst = [(xu.at[to], xg.at[me]), (xs, xall.at[me])][slot]
            copy = pltpu.make_async_remote_copy(
                src_ref=src, dst_ref=dst, send_sem=st_send.at[slot, d], recv_sem=st_recv.at[slot, d],
                device_id={"mem": to}, device_id_type=MESH,
            )
            copy.start()
            st_copies.append(copy)

    def localize(b):
        got = jnp.dot(
            three_parts(lrow[:, b * nobs:(b + 1) * nobs]), pick[b], preferred_element_type=F32
        )
        lcomp[b] = got[0:ndom] + got[ndom:2 * ndom] + got[2 * ndom:3 * ndom]

    def gather_prior(b):
        for copy in pri_copies[b]:
            copy.wait_recv()
        return jnp.concatenate([pbuf[b, i, m] for i in range(nmem) for m in range(own)], axis=0)

    observe(0)
    send_states(0)
    xg[me] = xu[me]

    for copy in loc_copies:
        copy.wait_recv()
    for t in range(ndom):
        lrow[t:t + 1, :] = lbuf[t]
    localize(0)
    for b in range(1, batches):
        prepare(b)

    def mixing_of(b, prior):
        value = comp[b, 6:7, :]
        error = comp[b, 7:8, :]
        error = jnp.where(error > 0.0, error, 1.0)
        mean = jnp.sum(prior, axis=0, keepdims=True) / members
        spread = prior - mean
        total = jnp.sum(spread * spread, axis=0, keepdims=True) / (members - 1) + error
        root = jnp.sqrt(total)
        gain = (value - mean) / total - spread / (root * (jnp.sqrt(error) + root))
        left, right = [], []
        for g in range(groups):
            local = jnp.concatenate(
                [gain[8 * g:8 * g + 8] * lcomp[b, t:t + 1, :] for t in range(ndom)], axis=0
            )
            placed = [jnp.zeros((g * members, cap), F32)] if g else []
            placed += [spread / (members - 1)]
            placed += [jnp.zeros((128 - (g + 1) * members, cap), F32)] if (g + 1) * members < 128 else []
            local_high, local_low = two_parts(local)
            placed_high, placed_low = two_parts(jnp.concatenate(placed, axis=0))
            left += [local_high, local_high, local_low]
            right += [placed_high, placed_low, placed_high]
        part = lax.dot_general(
            jnp.concatenate(left, axis=1), jnp.concatenate(right, axis=1), (((1,), (1,)), ((), ())),
            preferred_element_type=F32,
        )
        for t in range(ndom):
            ps[b, t] = part[8 * t:8 * t + 8]
        copies = []
        for d in range(ndom - 1, 0, -1):
            to = partner(tile, d, ndom)
            copy = pltpu.make_async_remote_copy(
                src_ref=ps.at[b, to], dst_ref=rb.at[b, tile],
                send_sem=mix_send.at[b, d], recv_sem=mix_recv.at[b, d],
                device_id={"dom": to}, device_id_type=MESH,
            )
            copy.start()
            copies.append(copy)
        rb[b, tile] = ps[b, tile]
        return copies

    def received(b, copies):
        for copy in copies:
            copy.wait_recv()
        got = jnp.sum(rb[b], axis=0)
        return jnp.concatenate([got[:, g * members:(g + 1) * members] for g in range(groups)], axis=0)

    eye = jnp.where(iota((members, members), 0) == iota((members, members), 1), 1.0, 0.0).astype(F32)
    mix_copies = []
    advance = eye
    folded = jnp.zeros((members, members), F32)
    for b in range(batches):
        prior = gather_prior(b)
        if b > 0:
            anomaly = prior - jnp.sum(prior, axis=0, keepdims=True) / members
            prior = prior + jnp.dot(folded, anomaly, precision=HIGHEST, preferred_element_type=F32)
        copies = mixing_of(b, prior)
        mix_copies += copies
        if b == 0:
            for later in range(1, batches):
                observe(later)
            send_states(1)
            xall[me] = xs[...]
            for later in range(1, batches):
                localize(later)
        mix = received(b, copies)
        folded = folded + (
            mix if b == 0 else jnp.dot(mix, advance, precision=HIGHEST, preferred_element_type=F32)
        )
        advance = eye + folded - jnp.sum(folded, axis=0, keepdims=True) / members
    weight = eye + folded - jnp.sum(folded, axis=1, keepdims=True) / members

    pairs = members * members
    choose = jnp.where(iota((pairs, members), 0) // members == iota((pairs, members), 1), 1.0, 0.0).astype(F32)
    spreadw = jnp.dot(choose, weight, precision=HIGHEST, preferred_element_type=F32)
    spreadw = jnp.where(iota((pairs, members), 0) % members == iota((pairs, members), 1), spreadw, 0.0)
    wb[...] = jnp.broadcast_to(jnp.sum(spreadw, axis=1, keepdims=True), (pairs, cols)).reshape(members, members, cols)

    for copy in st_copies[0:nmem - 1]:
        copy.wait_recv()

    def apply(to, dst):
        def one(i, carry):
            w = wb[to * own + i]
            acc = [jnp.zeros((8, wide), F32)] * rest
            for m in range(members):
                scale = jnp.broadcast_to(w[m:m + 1, 0:wide], (8, wide))
                for f in range(rest):
                    acc[f] = acc[f] + scale * xg[m // own, m % own, f]
            for f in range(rest):
                dst[to if dst is og else me, i, f] = acc[f]
            return carry

        lax.fori_loop(0, own, one, 0)

    fin_copies = []
    for d in range(nmem - 1, 0, -1):
        to = partner(me, d, nmem)
        apply(to, og)
        copy = pltpu.make_async_remote_copy(
            src_ref=og.at[to], dst_ref=og_in.at[me], send_sem=fin_send.at[d], recv_sem=fin_recv.at[d],
            device_id={"mem": to}, device_id_type=MESH,
        )
        copy.start()
        fin_copies.append(copy)
    apply(me, og_in)

    for copy in st_copies[nmem - 1:]:
        copy.wait_recv()

    def apply_gathered(i, carry):
        w = wb[me * own + i]
        for f in range(gathered):
            acc = jnp.zeros((rows, cols), F32)
            for m in range(members):
                acc = acc + jnp.broadcast_to(w[m:m + 1, :], (rows, cols)) * xall[m // own, m % own, f]
            for r in range(rows // 8):
                out_ref[r, i, f] = acc[8 * r:8 * r + 8]
        return carry

    lax.fori_loop(0, own, apply_gathered, 0)
    for copy in fin_copies:
        copy.wait_recv()
    for k in range(nmem):
        c = k % across * wide
        out_ref[k // across, :, gathered:, :, c:c + wide] = og_in[k]

    @pl.when(tile > 0)
    def _():
        for copy in down:
            copy.wait_send()

    @pl.when(tile < last)
    def _():
        for copy in up:
            copy.wait_send()

    for copy in loc_copies + sum(pri_copies, []) + st_copies + mix_copies + fin_copies:
        copy.wait_send()


def on_device(nmem, ndom, x, smooth, cross, obs_tile, place, field, obs_weights, values, variance, localization):
    own, fields, rows, cols = x.shape
    batches, nobs = place.shape
    cap = 2 * nobs // ndom
    members = own * nmem
    wide = rows * cols // (8 * nmem)
    rest = fields - GATHERED
    vmem = pl.BlockSpec(memory_space=pltpu.VMEM)
    anywhere = pl.BlockSpec(memory_space=pltpu.HBM)
    dma = pltpu.SemaphoreType.DMA
    bands = pl.pallas_call(
        functools.partial(kernel, nmem, ndom, cap),
        out_shape=jax.ShapeDtypeStruct((rows // 8, own, fields, 8, cols), F32),
        in_specs=[anywhere, anywhere, pl.BlockSpec(memory_space=pltpu.SMEM)] + [anywhere] * 7,
        out_specs=vmem,
        scratch_shapes=[
            pltpu.VMEM((batches * nobs // 128, 128), jnp.int32),
            pltpu.VMEM((batches, nobs), jnp.int32),
            pltpu.VMEM((batches, nobs), jnp.int32),
            pltpu.VMEM((batches, 4, nobs), F32),
            pltpu.VMEM((batches, nobs), F32),
            pltpu.VMEM((batches, nobs), F32),
            pltpu.VMEM((1, batches * nobs), F32),
            pltpu.VMEM((own, fields, rows + 2 * HALO, cols), F32),
            pltpu.VMEM((fields, rows + 2 * HALO, cols), F32),
            pltpu.VMEM((own, GATHERED, rows, cols), F32),
            pltpu.VMEM((nmem, own, GATHERED, rows, cols), F32),
            pltpu.VMEM((nmem, own, rest, 8, wide), F32),
            pltpu.VMEM((own, fields * rows, cols), BF16),
            pltpu.VMEM((own, fields * rows, cols), BF16),
            pltpu.VMEM((batches, nobs, cap), BF16),
            pltpu.VMEM((batches, 8, cap), F32),
            pltpu.VMEM((batches, 2, cols, cap), BF16),
            pltpu.VMEM((batches, 2, fields * rows, cap), F32),
            pltpu.VMEM((ndom, 1, batches * nobs), F32),
            pltpu.VMEM((ndom, batches * nobs), F32),
            pltpu.VMEM((batches, ndom, cap), F32),
            pltpu.VMEM((batches, nmem, own, 1, cap), F32),
            pltpu.VMEM((nmem, own, rest, 8, wide), F32),
            pltpu.VMEM((nmem, own, rest, 8, wide), F32),
            pltpu.VMEM((nmem, own, rest, 8, wide), F32),
            pltpu.VMEM((batches, ndom, 8, 128), F32),
            pltpu.VMEM((batches, ndom, 8, 128), F32),
            pltpu.VMEM((members, members, cols), F32),
            dma((9,)), dma((4,)), dma((4,)),
            dma((ndom,)), dma((ndom,)),
            dma((batches, nmem)), dma((batches, nmem)),
            dma((2, nmem)), dma((2, nmem)),
            dma((batches, ndom)), dma((batches, ndom)),
            dma((nmem,)), dma((nmem,)),
        ],
        compiler_params=pltpu.CompilerParams(
            collective_id=0, has_side_effects=True, vmem_limit_bytes=60 * 1024 * 1024
        ),
    )(
        x,
        smooth,
        cross,
        obs_tile.reshape(batches * nobs // 128, 128),
        place,
        field,
        jnp.transpose(obs_weights, (0, 2, 1)),
        values,
        variance,
        localization.reshape(1, batches * nobs),
    )
    return jnp.transpose(bands, (1, 2, 0, 3, 4)).reshape(own, fields, rows, cols)


def solution(mesh):
    placed = (
        P("mem", None, "dom", None),
        P(None, "dom", None),
        P(),
        P(),
        P(),
        P(),
        P(),
        P(),
        P(),
        P(None, "dom", None),
    )
    return jax.shard_map(
        functools.partial(on_device, mesh.shape["mem"], mesh.shape["dom"]),
        mesh=mesh,
        in_specs=placed,
        out_specs=P("mem", None, "dom", None),
        check_vma=False,
    )
```
